32 devices in a mesh: clips: 2 (over y), seq: 4 (over z), pair: 4 (over x, core).
Axes of the slice: x: 2, y: 2, z: 4, core: 2. Of those that a mesh axis runs over, the one named last changes fastest.
Arguments:
- queries: bfloat16 [4096, 5120], P(('clips', 'seq', 'pair')), parts along dimension 0, may hold values from -34 to 34
- key_rows: bfloat16 [4096, 5120], P(('clips', 'seq', 'pair')), parts along dimension 0, may hold values from -6 to 6
- value_rows: bfloat16 [4096, 5120], P(('clips', 'seq', 'pair')), parts along dimension 0, may hold values from -6 to 6
- block_lists: int32 [40, 16, 2], replicated, may hold values from 0 to 15, as said below
- block_counts: int32 [40, 16], replicated, may hold values from 1 to 2, as said below
Outputs:
- attended: bfloat16 [4096, 5120], P(('clips', 'seq', 'pair')), parts along dimension 0
The draws below stay inside these ranges and needn't reach their ends.
There are 2 independent parts, one for each index of `clips`. The reference program is written for one: setup_inputs(seed, part) draws one part's arguments, and reference() takes and returns one part's arrays. A program takes and returns all parts, laid end to end along the dimension named above; an argument that names none is the same for every part. Nothing has to cross between parts.
Inputs may be any that keep to these rules, and one draw needn't show every extreme that they name: `block_lists`: for each head and query block the entries are distinct and the first one is the query block itself; entries at positions block_counts[h, b] and beyond are not used. `block_counts`: some query block of some head has exactly 2 live key blocks.
All inputs are finite; a program needn't handle non-finite values.
Results may differ from the reference program's by a relative error of at most 0.0055.
Values may be sent and summed in bfloat16 or wider, within the bound.
A program may use at most 128 MiB of HBM per device.

```python
import math
import jax
import jax.numpy as jnp
from jax import lax

HEADS = 40
HD = 128
BLOCK = 128
NB = 16
TOKENS = 2048
MAXB = 2


def mask_parts(seed_key):
    base_key = jax.random.fold_in(seed_key, 29)
    head_key = jax.random.fold_in(base_key, 1)
    row_key = jax.random.fold_in(base_key, 2)
    pick_key = jax.random.fold_in(base_key, 3)
    busy_key = jax.random.fold_in(base_key, 4)
    order_key = jax.random.fold_in(base_key, 5)
    lowest = max(1, NB // 50)
    head_base = jax.random.randint(head_key, (HEADS,), lowest, MAXB + 1)
    busiest = jax.random.randint(busy_key, (), 0, HEADS)
    head_base = jnp.where(jnp.arange(HEADS, dtype=jnp.int32) == busiest, MAXB, head_base)
    floor_count = jnp.maximum(1, head_base // 2)
    raw_draw = jax.random.randint(row_key, (HEADS, NB), 0, 1 << 20)
    counts = floor_count[:, None] + raw_draw % (head_base - floor_count + 1)[:, None]
    pick_row = jax.random.randint(pick_key, (HEADS,), 0, NB)
    counts = jnp.where(jnp.arange(NB, dtype=jnp.int32)[None, :] == pick_row[:, None], head_base[:, None], counts)
    ranks = jax.random.randint(order_key, (HEADS, NB, NB), 0, 1 << 16) * NB + jnp.arange(NB, dtype=jnp.int32)[None, None, :]
    diagonal = jnp.arange(NB, dtype=jnp.int32)[:, None] == jnp.arange(NB, dtype=jnp.int32)[None, :]
    ranks = jnp.where(diagonal[None, :, :], (1 << 16) * NB + NB, ranks)
    lists = lax.top_k(ranks, MAXB)[1].astype(jnp.int32)
    return (lists, counts.astype(jnp.int32))


def draw_queries(key, part):
    full_shape = (TOKENS, HEADS * HD)
    sample = jnp.clip(jax.random.normal(jax.random.fold_in(key, 13), full_shape, jnp.float32), -6.0, 6.0)
    return sample.astype(jnp.bfloat16)


def draw_key_rows(key, part):
    full_shape = (TOKENS, HEADS * HD)
    sample = jnp.clip(jax.random.normal(jax.random.fold_in(key, 17), full_shape, jnp.float32), -6.0, 6.0)
    return sample.astype(jnp.bfloat16)


def draw_block_lists(key, part):
    lists, counts = mask_parts(key)
    return lists


def draw_block_counts(key, part):
    lists, counts = mask_parts(key)
    return counts


def shard_levels(rng, extent, cuts, least, largest):
    factor_of = 1.0
    for position, shards_of in cuts:
        steps = jax.random.uniform(jax.random.fold_in(jax.random.fold_in(rng, 6), position), (shards_of,), jnp.float32, least / len(cuts), largest / len(cuts))
        factor_of = factor_of * jnp.repeat(jnp.exp(steps), extent[position] // shards_of).reshape((-1,) + (1,) * (len(extent) - 1 - position))
    return factor_of


def centred(own_key, extent, scale, limit, shards=(), kind=jnp.bfloat16):
    drawn = jax.random.normal(own_key, extent, jnp.float32) * scale
    if len(shards) > 0:
        drawn = shard_levels(own_key, extent, shards, -0.22, 0.18) * drawn
    return jnp.clip(drawn, min=-limit, max=limit).astype(kind)


def setup_inputs(seed: int = 0, part: int = 0) -> dict:
    splits = jax.random.split(jax.random.key(seed), 6)
    part_splits = jax.random.split(jax.random.fold_in(splits[5], part), 6)
    queries = draw_queries(jax.random.fold_in(jax.random.fold_in(splits[5], part), 71), part)
    key_rows = draw_key_rows(jax.random.fold_in(jax.random.fold_in(splits[5], part), 71), part)
    value_rows = centred(part_splits[2], (TOKENS, HEADS * HD), 1.0, 6.0, ((0, 16),))
    block_lists = draw_block_lists(jax.random.fold_in(splits[5], 71), part)
    block_counts = draw_block_counts(jax.random.fold_in(splits[5], 71), part)
    return {"queries": queries, "key_rows": key_rows, "value_rows": value_rows, "block_lists": block_lists, "block_counts": block_counts}


def reference(queries, key_rows, value_rows, block_lists, block_counts):
    score_scale = 1.0 / math.sqrt(HD)

    def one_head(head_id):
        col_start = head_id * HD
        head_query = lax.dynamic_slice_in_dim(queries, col_start, HD, 1).reshape(NB, BLOCK, HD)
        head_key = lax.dynamic_slice_in_dim(key_rows, col_start, HD, 1).reshape(NB, BLOCK, HD)
        head_value = lax.dynamic_slice_in_dim(value_rows, col_start, HD, 1).reshape(NB, BLOCK, HD)
        own_lists = block_lists[head_id]
        own_counts = block_counts[head_id]
        key_gathered = head_key[own_lists]
        value_gathered = head_value[own_lists]
        scores = jnp.einsum('nad,nmbd->namb', head_query.astype(jnp.float32), key_gathered.astype(jnp.float32)) * score_scale
        live_mask = (jnp.arange(MAXB, dtype=jnp.int32)[None, :] < own_counts[:, None])[:, None, :, None]
        row_max = lax.optimization_barrier(jnp.max(jnp.where(live_mask, scores, -jnp.inf), axis=(2, 3), keepdims=True))
        raised = jnp.where(live_mask, jnp.exp(scores - row_max), 0.0)
        total = lax.optimization_barrier(jnp.sum(raised, axis=(2, 3)))
        weights = raised.astype(jnp.bfloat16)
        mixed_out = jnp.einsum('namb,nmbd->nad', weights.astype(jnp.float32), value_gathered.astype(jnp.float32))
        return (mixed_out / total[:, :, None]).astype(jnp.bfloat16)
    heads_out = lax.map(one_head, jnp.arange(HEADS, dtype=jnp.int32))
    return heads_out.transpose(1, 2, 0, 3).reshape(TOKENS, HEADS * HD)
```

```python
import functools
import math

import jax
import jax.numpy as jnp
from jax import lax
from jax.experimental import pallas as pl
from jax.experimental.pallas import tpu as pltpu
from jax.sharding import PartitionSpec as P

HEADS = 40
HD = 128
BLOCK = 128
MESH = pl.DeviceIdType.MESH
SLOT_CHOICES = (20, 24, 40)
SCALE = 1.0 / math.sqrt(HD)


def attend(query, key, value, live):
    scores = (
        lax.dot_general(
            query, key, (((1,), (1,)), ((), ())), preferred_element_type=jnp.float32
        )
        * SCALE
    )
    if live is not None:
        scores = jnp.where(live, scores, -1e30)
    raised = jnp.exp(scores - jnp.max(scores, axis=1, keepdims=True))
    total = jnp.sum(raised, axis=1, keepdims=True)
    mixed = jnp.dot(raised.astype(jnp.bfloat16), value, preferred_element_type=jnp.float32)
    return (mixed / total).astype(jnp.bfloat16)


def columns(head):
    return pl.ds(pl.multiple_of(head * HD, HD), HD)


def pack_kernel(slots, order_ref, q_ref, k_ref, v_ref, packed):
    def pack(slot, carry):
        cols = columns(order_ref[slot])
        packed[slot, 0] = q_ref[:, cols]
        packed[slot, 1] = k_ref[:, cols]
        packed[slot, 2] = v_ref[:, cols]
        return carry

    lax.fori_loop(0, slots, pack, 0)


def place_kernel(place_ref, alone_ref, returned, out_ref):
    def place(head, carry):
        at = place_ref[head]
        cols = columns(head)
        got = returned[jnp.maximum(at, 0)]
        out_ref[:, cols] = jnp.where(at >= 0, got, alone_ref[:, cols])
        return carry

    lax.fori_loop(0, HEADS, place, 0)


def kernel(
    slots,
    seq_count,
    pair_count,
    most,
    lists_ref,
    counts_ref,
    q_ref,
    k_ref,
    v_ref,
    packed,
    alone_ref,
    returned,
    mixed,
    send_sem,
    recv_sem,
    mixed_sem,
    returned_sem,
    *landed,
):
    group = seq_count * pair_count
    half = group // 2
    rounds = -(-slots // half)
    clip = lax.axis_index("clips")
    me = lax.axis_index("seq") * pair_count + lax.axis_index("pair")
    side = me // half
    within = me % half
    turn = (within % (half // 2)) * 2 + within // (half // 2)

    def device(place):
        return (clip, place // pair_count, place % pair_count)

    def keeper(lane):
        return (lane % 2) * (half // 2) + lane // 2

    barrier = pltpu.get_barrier_semaphore()

    def greet(step, carry):
        pl.semaphore_signal(
            barrier, inc=1, device_id=device((me + step) % group), device_id_type=MESH
        )
        return carry

    lax.fori_loop(1, group, greet, 0)
    pl.semaphore_wait(barrier, group - 1)

    def far_copy(slot, row, owner):
        return pltpu.make_async_remote_copy(
            src_ref=packed.at[slot, pl.ds(1, 2)],
            dst_ref=landed[row].at[me, pl.ds(1, 2)],
            send_sem=send_sem.at[slot, 0],
            recv_sem=recv_sem.at[row, me],
            device_id=device(owner),
            device_id_type=MESH,
        )

    def near_copy(slot, row, owner):
        return pltpu.make_async_remote_copy(
            src_ref=packed.at[slot],
            dst_ref=landed[row].at[me],
            send_sem=send_sem.at[slot, 1],
            recv_sem=recv_sem.at[row, me],
            device_id=device(owner),
            device_id_type=MESH,
        )

    for row in range(rounds):
        width = min(half, slots - row * half)

        def give(step, carry, row=row, width=width):
            lane = (step + me) % width
            slot = row * half + lane
            far = (1 - side) * half + keeper(lane)
            near = side * half + keeper(lane)
            far_copy(slot, row, far).start()

            @pl.when(near != me)
            def _():
                near_copy(slot, row, near).start()

            @pl.when(near == me)
            def _():
                pltpu.make_async_copy(
                    packed.at[slot], landed[row].at[me], recv_sem.at[row, me]
                ).start()

            return carry

        lax.fori_loop(0, width, give, 0)

    def alone(head, carry):
        cols = columns(head)
        alone_ref[:, cols] = attend(q_ref[:, cols], k_ref[:, cols], v_ref[:, cols], None)
        return carry

    lax.fori_loop(0, HEADS, alone, 0)

    spot = lax.broadcasted_iota(jnp.int32, (BLOCK, most * BLOCK), 1)

    def back_copy(row, slot, near):
        return pltpu.make_async_remote_copy(
            src_ref=mixed.at[row, near],
            dst_ref=returned.at[slot],
            send_sem=mixed_sem.at[row, near],
            recv_sem=returned_sem.at[slot],
            device_id=device(side * half + near),
            device_id_type=MESH,
        )

    for row in range(rounds):
        slot = row * half + turn

        @pl.when(slot < slots)
        def _(row=row, slot=slot):
            def near_in(step, carry):
                source = side * half + step
                pltpu.make_async_copy(
                    landed[row].at[source], landed[row].at[source], recv_sem.at[row, source]
                ).wait()
                return carry

            lax.fori_loop(0, half, near_in, 0)

            def far_in(step, carry):
                source = (1 - side) * half + step
                got = landed[row].at[source, pl.ds(1, 2)]
                pltpu.make_async_copy(got, got, recv_sem.at[row, source]).wait()
                return carry

            lax.fori_loop(0, half, far_in, 0)

            def work(step, carry):
                near = (step + within + 1) % half
                block = side * half + near
                entry = slot * group + block
                keys = []
                values = []
                for position in range(most):
                    pick = lists_ref[entry * most + position]
                    keys.append(landed[row][pick, 1])
                    values.append(landed[row][pick, 2])
                mixed[row, near] = attend(
                    landed[row][block, 0],
                    jnp.concatenate(keys, axis=0),
                    jnp.concatenate(values, axis=0),
                    spot < counts_ref[entry] * BLOCK,
                )

                @pl.when(near != within)
                def _():
                    back_copy(row, slot, near).start()

                @pl.when(near == within)
                def _():
                    pltpu.make_async_copy(
                        mixed.at[row, near], returned.at[slot], returned_sem.at[slot]
                    ).start()

                return carry

            lax.fori_loop(0, half, work, 0)

    def come(slot, carry):
        pltpu.make_async_copy(returned.at[slot], returned.at[slot], returned_sem.at[slot]).wait()
        return carry

    lax.fori_loop(0, slots, come, 0)

    for row in range(rounds):
        width = min(half, slots - row * half)

        def sent(lane, carry, row=row):
            slot = row * half + lane
            far = (1 - side) * half + keeper(lane)
            near = side * half + keeper(lane)
            far_copy(slot, row, far).wait_send()

            @pl.when(near != me)
            def _():
                near_copy(slot, row, near).wait_send()

            return carry

        lax.fori_loop(0, width, sent, 0)

        @pl.when(row * half + turn < slots)
        def _(row=row):
            def gone(step, carry):
                near = (step + within + 1) % half
                back_copy(row, row * half + turn, near).wait_send()
                return carry

            lax.fori_loop(0, half - 1, gone, 0)


def exchange(slots, number, seq_count, pair_count, most, tables, rows):
    group = seq_count * pair_count
    half = group // 2
    rounds = -(-slots // half)
    smem = pl.BlockSpec(memory_space=pltpu.SMEM)
    vmem = pl.BlockSpec(memory_space=pltpu.VMEM)
    bf16 = jnp.bfloat16
    order, place, lists, counts = tables
    whole_rows = jax.ShapeDtypeStruct((BLOCK, HEADS * HD), bf16)
    packed = pl.pallas_call(
        functools.partial(pack_kernel, slots),
        out_shape=jax.ShapeDtypeStruct((slots, 3, BLOCK, HD), bf16),
        in_specs=[smem] + [vmem] * 3,
        out_specs=vmem,
        compiler_params=pltpu.CompilerParams(vmem_limit_bytes=32 << 20),
    )(order, *rows)
    alone, returned = pl.pallas_call(
        functools.partial(kernel, slots, seq_count, pair_count, most),
        out_shape=(whole_rows, jax.ShapeDtypeStruct((slots, BLOCK, HD), bf16)),
        in_specs=[smem] * 2 + [vmem] * 3 + [pl.BlockSpec(memory_space=pl.ANY)],
        out_specs=(vmem, vmem),
        scratch_shapes=[
            pltpu.VMEM((rounds, half, BLOCK, HD), bf16),
            pltpu.SemaphoreType.DMA((slots, 2)),
            pltpu.SemaphoreType.DMA((rounds, group)),
            pltpu.SemaphoreType.DMA((rounds, half)),
            pltpu.SemaphoreType.DMA((slots,)),
        ]
        + [pltpu.VMEM((group, 3, BLOCK, HD), bf16)] * rounds,
        compiler_params=pltpu.CompilerParams(
            collective_id=number, has_side_effects=True, vmem_limit_bytes=48 << 20
        ),
    )(lists, counts, *rows, packed)
    return pl.pallas_call(
        place_kernel,
        out_shape=whole_rows,
        in_specs=[smem] + [vmem] * 2,
        out_specs=vmem,
        compiler_params=pltpu.CompilerParams(vmem_limit_bytes=32 << 20),
    )(place, alone, returned)


def body(queries, key_rows, value_rows, block_lists, block_counts):
    seq_count = lax.axis_size("seq")
    pair_count = lax.axis_size("pair")
    group = seq_count * pair_count
    most = block_lists.shape[2]
    heads = jnp.arange(HEADS, dtype=jnp.int32)
    active = jnp.max(block_counts, axis=1) > 1
    before = jnp.sum(
        jnp.where((heads[None, :] < heads[:, None]) & active[None, :], 1, 0), axis=1
    )
    place = jnp.where(active, before, -1).astype(jnp.int32)
    order = jnp.sum(
        jnp.where(place[None, :] == heads[:, None], heads[None, :], 0), axis=1
    ).astype(jnp.int32)
    filled = jnp.sum(active.astype(jnp.int32))
    position = jnp.arange(most, dtype=jnp.int32)
    own = jnp.arange(group, dtype=jnp.int32)
    lists = jnp.where(
        position[None, None, :] < block_counts[:, :, None], block_lists, own[None, :, None]
    ).reshape(HEADS, group * most)
    picked = (place[None, :] == heads[:, None])[:, :, None]
    slot_lists = jnp.sum(jnp.where(picked, lists[None], 0), axis=1).astype(jnp.int32)
    slot_counts = jnp.sum(jnp.where(picked, block_counts[None], 0), axis=1).astype(jnp.int32)
    tables = (order, place, slot_lists.reshape(-1), jnp.maximum(slot_counts, 1).reshape(-1))
    branch = sum((filled > slots).astype(jnp.int32) for slots in SLOT_CHOICES[:-1])
    return lax.switch(
        branch,
        [
            functools.partial(exchange, slots, number, seq_count, pair_count, most)
            for number, slots in enumerate(SLOT_CHOICES)
        ],
        tables,
        (queries, key_rows, value_rows),
    )


def solution(mesh):
    placed = P(("clips", "seq", "pair"), None)
    return jax.shard_map(
        body,
        mesh=mesh,
        in_specs=(placed, placed, placed, P(), P()),
        out_specs=placed,
        check_vma=False,
    )
```

```python
import functools
import math

import jax
import jax.numpy as jnp
from jax import lax
from jax.experimental import pallas as pl
from jax.experimental.pallas import tpu as pltpu
from jax.sharding import PartitionSpec as P

HEADS = 40
HD = 128
BLOCK = 128
MESH = pl.DeviceIdType.MESH
SLOT_CHOICES = (16, 18, 20, 22, 24, 28, 40)
SCALE = 1.0 / math.sqrt(HD)


def attend(query, key, value, live):
    scores = (
        lax.dot_general(
            query, key, (((1,), (1,)), ((), ())), preferred_element_type=jnp.float32
        )
        * SCALE
    )
    if live is not None:
        scores = jnp.where(live, scores, -1e30)
    raised = jnp.exp(scores - jnp.max(scores, axis=1, keepdims=True))
    total = jnp.sum(raised, axis=1, keepdims=True)
    mixed = jnp.dot(raised.astype(jnp.bfloat16), value, preferred_element_type=jnp.float32)
    return (mixed / total).astype(jnp.bfloat16)


def columns(head):
    return pl.ds(pl.multiple_of(head * HD, HD), HD)


def pack_kernel(slots, order_ref, q_ref, k_ref, v_ref, packed):
    def pack(slot, carry):
        cols = columns(order_ref[slot])
        packed[slot, 0] = q_ref[:, cols]
        packed[slot, 1] = k_ref[:, cols]
        packed[slot, 2] = v_ref[:, cols]
        return carry

    lax.fori_loop(0, slots, pack, 0)


def place_kernel(place_ref, alone_ref, returned, out_ref):
    def place(head, carry):
        at = place_ref[head]
        cols = columns(head)
        got = returned[jnp.maximum(at, 0)]
        out_ref[:, cols] = jnp.where(at >= 0, got, alone_ref[:, cols])
        return carry

    lax.fori_loop(0, HEADS, place, 0)


def kernel(
    slots,
    seq_count,
    pair_count,
    most,
    order_ref,
    lists_ref,
    counts_ref,
    q_ref,
    k_ref,
    v_ref,
    packed,
    alone_ref,
    returned,
    mixed,
    send_sem,
    recv_sem,
    mixed_sem,
    returned_sem,
    *landed,
):
    group = seq_count * pair_count
    half = group // 2
    rounds = -(-slots // half)
    clip = lax.axis_index("clips")
    me = lax.axis_index("seq") * pair_count + lax.axis_index("pair")
    side = me // half
    within = me % half
    turn = (within % (half // 2)) * 2 + within // (half // 2)

    def device(place):
        return (clip, place // pair_count, place % pair_count)

    def keeper(lane):
        return (lane % 2) * (half // 2) + lane // 2

    barrier = pltpu.get_barrier_semaphore()

    def greet(step, carry):
        pl.semaphore_signal(
            barrier, inc=1, device_id=device((me + step) % group), device_id_type=MESH
        )
        return carry

    lax.fori_loop(1, group, greet, 0)
    pl.semaphore_wait(barrier, group - 1)

    def far_copy(slot, row, owner):
        return pltpu.make_async_remote_copy(
            src_ref=packed.at[slot, pl.ds(1, 2)],
            dst_ref=landed[row].at[me, pl.ds(1, 2)],
            send_sem=send_sem.at[slot, 0],
            recv_sem=recv_sem.at[row, me],
            device_id=device(owner),
            device_id_type=MESH,
        )

    def near_copy(slot, row, owner):
        return pltpu.make_async_remote_copy(
            src_ref=packed.at[slot],
            dst_ref=landed[row].at[me],
            send_sem=send_sem.at[slot, 1],
            recv_sem=recv_sem.at[row, me],
            device_id=device(owner),
            device_id_type=MESH,
        )

    for row in range(rounds):
        width = min(half, slots - row * half)

        def give(step, carry, row=row, width=width):
            lane = (step + me) % width
            slot = row * half + lane
            far = (1 - side) * half + keeper(lane)
            near = side * half + keeper(lane)
            far_copy(slot, row, far).start()

            @pl.when(near != me)
            def _():
                near_copy(slot, row, near).start()

            @pl.when(near == me)
            def _():
                pltpu.make_async_copy(
                    packed.at[slot], landed[row].at[me], recv_sem.at[row, me]
                ).start()

            return carry

        lax.fori_loop(0, width, give, 0)

    def alone(head, carry):
        cols = columns(head)
        alone_ref[:, cols] = attend(q_ref[:, cols], k_ref[:, cols], v_ref[:, cols], None)
        return carry

    lax.fori_loop(0, HEADS, alone, 0, unroll=4)

    spot = lax.broadcasted_iota(jnp.int32, (BLOCK, most * BLOCK), 1)

    def back_copy(row, slot, near):
        return pltpu.make_async_remote_copy(
            src_ref=mixed.at[row, near],
            dst_ref=returned.at[slot],
            send_sem=mixed_sem.at[row, near],
            recv_sem=returned_sem.at[slot],
            device_id=device(side * half + near),
            device_id_type=MESH,
        )

    for row in range(rounds):
        slot = row * half + turn

        @pl.when(slot < slots)
        def _(row=row, slot=slot):
            def near_in(step, carry):
                source = side * half + step
                pltpu.make_async_copy(
                    landed[row].at[source], landed[row].at[source], recv_sem.at[row, source]
                ).wait()
                return carry

            lax.fori_loop(0, half, near_in, 0)

            def far_in(step, carry):
                source = (1 - side) * half + step
                got = landed[row].at[source, pl.ds(1, 2)]
                pltpu.make_async_copy(got, got, recv_sem.at[row, source]).wait()
                return carry

            lax.fori_loop(0, half, far_in, 0)

            head = order_ref[slot]

            def work(step, carry):
                near = (step + within + 1) % half
                block = side * half + near
                entry = head * group + block
                keys = []
                values = []
                for position in range(most):
                    pick = lists_ref[entry * most + position]
                    keys.append(landed[row][pick, 1])
                    values.append(landed[row][pick, 2])
                mixed[row, near] = attend(
                    landed[row][block, 0],
                    jnp.concatenate(keys, axis=0),
                    jnp.concatenate(values, axis=0),
                    spot < counts_ref[entry] * BLOCK,
                )

                @pl.when(near != within)
                def _():
                    back_copy(row, slot, near).start()

                @pl.when(near == within)
                def _():
                    pltpu.make_async_copy(
                        mixed.at[row, near], returned.at[slot], returned_sem.at[slot]
                    ).start()

                return carry

            lax.fori_loop(0, half, work, 0, unroll=4)

    def come(slot, carry):
        pltpu.make_async_copy(returned.at[slot], returned.at[slot], returned_sem.at[slot]).wait()
        return carry

    lax.fori_loop(0, slots, come, 0)

    for row in range(rounds):
        width = min(half, slots - row * half)

        def sent(lane, carry, row=row):
            slot = row * half + lane
            far = (1 - side) * half + keeper(lane)
            near = side * half + keeper(lane)
            far_copy(slot, row, far).wait_send()

            @pl.when(near != me)
            def _():
                near_copy(slot, row, near).wait_send()

            return carry

        lax.fori_loop(0, width, sent, 0)

        @pl.when(row * half + turn < slots)
        def _(row=row):
            def gone(step, carry):
                near = (step + within + 1) % half
                back_copy(row, row * half + turn, near).wait_send()
                return carry

            lax.fori_loop(0, half - 1, gone, 0)


def exchange(slots, number, seq_count, pair_count, most, tables, rows):
    group = seq_count * pair_count
    half = group // 2
    rounds = -(-slots // half)
    smem = pl.BlockSpec(memory_space=pltpu.SMEM)
    vmem = pl.BlockSpec(memory_space=pltpu.VMEM)
    bf16 = jnp.bfloat16
    order, place, lists, counts = tables
    whole_rows = jax.ShapeDtypeStruct((BLOCK, HEADS * HD), bf16)
    packed = pl.pallas_call(
        functools.partial(pack_kernel, slots),
        out_shape=jax.ShapeDtypeStruct((slots, 3, BLOCK, HD), bf16),
        in_specs=[smem] + [vmem] * 3,
        out_specs=vmem,
        compiler_params=pltpu.CompilerParams(vmem_limit_bytes=32 << 20),
    )(order, *rows)
    alone, returned = pl.pallas_call(
        functools.partial(kernel, slots, seq_count, pair_count, most),
        out_shape=(whole_rows, jax.ShapeDtypeStruct((slots, BLOCK, HD), bf16)),
        in_specs=[smem] * 3 + [vmem] * 3 + [pl.BlockSpec(memory_space=pl.ANY)],
        out_specs=(vmem, vmem),
        scratch_shapes=[
            pltpu.VMEM((rounds, half, BLOCK, HD), bf16),
            pltpu.SemaphoreType.DMA((slots, 2)),
            pltpu.SemaphoreType.DMA((rounds, group)),
            pltpu.SemaphoreType.DMA((rounds, half)),
            pltpu.SemaphoreType.DMA((slots,)),
        ]
        + [pltpu.VMEM((group, 3, BLOCK, HD), bf16)] * rounds,
        compiler_params=pltpu.CompilerParams(
            collective_id=number, has_side_effects=True, vmem_limit_bytes=48 << 20
        ),
    )(order, lists, counts, *rows, packed)
    return pl.pallas_call(
        place_kernel,
        out_shape=whole_rows,
        in_specs=[smem] + [vmem] * 2,
        out_specs=vmem,
        compiler_params=pltpu.CompilerParams(vmem_limit_bytes=32 << 20),
    )(place, alone, returned)


def body(queries, key_rows, value_rows, block_lists, block_counts):
    seq_count = lax.axis_size("seq")
    pair_count = lax.axis_size("pair")
    group = seq_count * pair_count
    most = block_lists.shape[2]
    heads = jnp.arange(HEADS, dtype=jnp.int32)
    active = jnp.max(block_counts, axis=1) > 1
    before = jnp.sum(
        jnp.where((heads[None, :] < heads[:, None]) & active[None, :], 1, 0), axis=1
    )
    place = jnp.where(active, before, -1).astype(jnp.int32)
    order = jnp.sum(
        jnp.where(place[None, :] == heads[:, None], heads[None, :], 0), axis=1
    ).astype(jnp.int32)
    filled = jnp.sum(active.astype(jnp.int32))
    tables = (order, place, block_lists.reshape(-1), block_counts.reshape(-1))
    branch = sum((filled > slots).astype(jnp.int32) for slots in SLOT_CHOICES[:-1])
    return lax.switch(
        branch,
        [
            functools.partial(exchange, slots, number, seq_count, pair_count, most)
            for number, slots in enumerate(SLOT_CHOICES)
        ],
        tables,
        (queries, key_rows, value_rows),
    )


def solution(mesh):
    placed = P(("clips", "seq", "pair"), None)
    return jax.shard_map(
        body,
        mesh=mesh,
        in_specs=(placed, placed, placed, P(), P()),
        out_specs=placed,
        check_vma=False,
    )
```

```python
import functools
import math

import jax
import jax.numpy as jnp
from jax import lax
from jax.experimental import pallas as pl
from jax.experimental.pallas import tpu as pltpu
from jax.sharding import PartitionSpec as P

HEADS = 40
HD = 128
BLOCK = 128
MESH = pl.DeviceIdType.MESH
SLOT_CHOICES = (14, 16, 18, 19, 20, 21, 22, 23, 24, 26, 28, 40)
SCALE = 1.0 / math.sqrt(HD)


def attend(query, key, value, live):
    scores = (
        lax.dot_general(
            query, key, (((1,), (1,)), ((), ())), preferred_element_type=jnp.float32
        )
        * SCALE
    )
    if live is not None:
        scores = jnp.where(live, scores, -1e30)
    raised = jnp.exp(scores - jnp.max(scores, axis=1, keepdims=True))
    total = jnp.sum(raised, axis=1, keepdims=True)
    mixed = jnp.dot(raised.astype(jnp.bfloat16), value, preferred_element_type=jnp.float32)
    return (mixed / total).astype(jnp.bfloat16)


def columns(head):
    return pl.ds(pl.multiple_of(head * HD, HD), HD)


def pack_kernel(slots, order_ref, q_ref, k_ref, v_ref, packed, sem):
    def copies(slot):
        cols = columns(order_ref[slot])
        return [
            pltpu.make_async_copy(ref.at[:, cols], packed.at[slot, part], sem.at[slot, part])
            for part, ref in enumerate((q_ref, k_ref, v_ref))
        ]

    def begin(slot, carry):
        for copy in copies(slot):
            copy.start()
        return carry

    def finish(slot, carry):
        for copy in copies(slot):
            copy.wait()
        return carry

    lax.fori_loop(0, slots, begin, 0)
    lax.fori_loop(0, slots, finish, 0)


def kernel(
    slots,
    seq_count,
    pair_count,
    most,
    order_ref,
    place_ref,
    *refs,
):
    picks = refs[: most - 1]
    (
        q_hbm,
        k_hbm,
        v_hbm,
        packed,
        out_ref,
        q_ref,
        k_ref,
        v_ref,
        own_sem,
        returned,
        mixed,
        send_sem,
        recv_sem,
        mixed_sem,
        returned_sem,
        *landed,
    ) = refs[most - 1 :]
    group = seq_count * pair_count
    half = group // 2
    rounds = -(-slots // half)
    clip = lax.axis_index("clips")
    me = lax.axis_index("seq") * pair_count + lax.axis_index("pair")
    side = me // half
    within = me % half
    crossed = half == 8 and pair_count == 4
    if crossed:
        plane, across = within // 4, within // 2 % 2
        turn = plane + 2 * ((plane + across) % 2) + 4 * (within % 2)
    else:
        turn = (within % (half // 2)) * 2 + within // (half // 2)

    def device(place):
        return (clip, place // pair_count, place % pair_count)

    def keeper(lane):
        if crossed:
            return (lane % 2) * 4 + (lane + lane // 2) % 2 * 2 + lane // 4
        return (lane % 2) * (half // 2) + lane // 2

    own_copies = [
        pltpu.make_async_copy(source, target, own_sem.at[part])
        for part, (source, target) in enumerate(((q_hbm, q_ref), (k_hbm, k_ref), (v_hbm, v_ref)))
    ]
    barrier = pltpu.get_barrier_semaphore()

    def greet(step, carry):
        pl.semaphore_signal(
            barrier, inc=1, device_id=device((me + step) % group), device_id_type=MESH
        )
        return carry

    lax.fori_loop(1, group, greet, 0)
    pl.semaphore_wait(barrier, group - 1)

    def far_copy(slot, row, owner):
        return pltpu.make_async_remote_copy(
            src_ref=packed.at[slot, pl.ds(1, 2)],
            dst_ref=landed[row].at[me, pl.ds(1, 2)],
            send_sem=send_sem.at[slot, 0],
            recv_sem=recv_sem.at[row, me],
            device_id=device(owner),
            device_id_type=MESH,
        )

    def near_copy(slot, row, owner):
        return pltpu.make_async_remote_copy(
            src_ref=packed.at[slot],
            dst_ref=landed[row].at[me],
            send_sem=send_sem.at[slot, 1],
            recv_sem=recv_sem.at[row, me],
            device_id=device(owner),
            device_id_type=MESH,
        )

    for row in range(rounds):
        width = min(half, slots - row * half)

        def give(step, carry, row=row, width=width):
            lane = (step + me) % width
            slot = row * half + lane
            far = (1 - side) * half + keeper(lane)
            near = side * half + keeper(lane)
            far_copy(slot, row, far).start()

            @pl.when(near != me)
            def _():
                near_copy(slot, row, near).start()

            @pl.when(near == me)
            def _():
                pltpu.make_async_copy(
                    packed.at[slot], landed[row].at[me], recv_sem.at[row, me]
                ).start()

            return carry

        lax.fori_loop(0, width, give, 0)

    for copy in own_copies:
        copy.start()
    for copy in own_copies:
        copy.wait()

    def alone(head, carry):
        cols = columns(head)
        out_ref[:, cols] = attend(q_ref[:, cols], k_ref[:, cols], v_ref[:, cols], None)
        return carry

    lax.fori_loop(0, HEADS, alone, 0, unroll=4)

    spot = lax.broadcasted_iota(jnp.int32, (BLOCK, most * BLOCK), 1)

    def back_copy(row, slot, near):
        return pltpu.make_async_remote_copy(
            src_ref=mixed.at[row, near],
            dst_ref=returned.at[slot],
            send_sem=mixed_sem.at[row, near],
            recv_sem=returned_sem.at[slot],
            device_id=device(side * half + near),
            device_id_type=MESH,
        )

    for row in range(rounds):
        slot = row * half + turn

        @pl.when(slot < slots)
        def _(row=row, slot=slot):
            def near_in(step, carry):
                source = side * half + step
                pltpu.make_async_copy(
                    landed[row].at[source], landed[row].at[source], recv_sem.at[row, source]
                ).wait()
                return carry

            lax.fori_loop(0, half, near_in, 0)

            def far_in(step, carry):
                source = (1 - side) * half + step
                got = landed[row].at[source, pl.ds(1, 2)]
                pltpu.make_async_copy(got, got, recv_sem.at[row, source]).wait()
                return carry

            lax.fori_loop(0, half, far_in, 0)

            head = order_ref[slot]

            def work(step, carry):
                near = (step + within + 1) % half
                block = side * half + near
                keys = [landed[row][block, 1]]
                values = [landed[row][block, 2]]
                live = 1
                for pick_ref in picks:
                    pick = pick_ref[block, head]
                    live += jnp.where(pick >= 0, 1, 0)
                    keys.append(landed[row][jnp.maximum(pick, 0), 1])
                    values.append(landed[row][jnp.maximum(pick, 0), 2])
                mixed[row, near] = attend(
                    landed[row][block, 0],
                    jnp.concatenate(keys, axis=0),
                    jnp.concatenate(values, axis=0),
                    spot < live * BLOCK,
                )

                @pl.when(near != within)
                def _():
                    back_copy(row, slot, near).start()

                @pl.when(near == within)
                def _():
                    pltpu.make_async_copy(
                        mixed.at[row, near], returned.at[slot], returned_sem.at[slot]
                    ).start()

                return carry

            lax.fori_loop(0, half, work, 0, unroll=4)

    def come(slot, carry):
        pltpu.make_async_copy(returned.at[slot], returned.at[slot], returned_sem.at[slot]).wait()
        return carry

    lax.fori_loop(0, slots, come, 0)

    def place(head, carry):
        at = place_ref[head]
        cols = columns(head)
        out_ref[:, cols] = jnp.where(at >= 0, returned[jnp.maximum(at, 0)], out_ref[:, cols])
        return carry

    lax.fori_loop(0, HEADS, place, 0, unroll=4)

    for row in range(rounds):
        width = min(half, slots - row * half)

        def sent(lane, carry, row=row):
            slot = row * half + lane
            far = (1 - side) * half + keeper(lane)
            near = side * half + keeper(lane)
            far_copy(slot, row, far).wait_send()

            @pl.when(near != me)
            def _():
                near_copy(slot, row, near).wait_send()

            return carry

        lax.fori_loop(0, width, sent, 0)

        @pl.when(row * half + turn < slots)
        def _(row=row):
            def gone(step, carry):
                near = (step + within + 1) % half
                back_copy(row, row * half + turn, near).wait_send()
                return carry

            lax.fori_loop(0, half - 1, gone, 0)


def exchange(slots, number, seq_count, pair_count, most, tables, rows):
    group = seq_count * pair_count
    half = group // 2
    rounds = -(-slots // half)
    smem = pl.BlockSpec(memory_space=pltpu.SMEM)
    vmem = pl.BlockSpec(memory_space=pltpu.VMEM)
    bf16 = jnp.bfloat16
    anywhere = pl.BlockSpec(memory_space=pl.ANY)
    order, place, *picks = tables
    packed = pl.pallas_call(
        functools.partial(pack_kernel, slots),
        out_shape=jax.ShapeDtypeStruct((slots, 3, BLOCK, HD), bf16),
        in_specs=[smem] + [anywhere] * 3,
        out_specs=anywhere,
        scratch_shapes=[pltpu.SemaphoreType.DMA((slots, 3))],
        compiler_params=pltpu.CompilerParams(vmem_limit_bytes=60 << 20),
    )(order, *rows)
    return pl.pallas_call(
        functools.partial(kernel, slots, seq_count, pair_count, most),
        out_shape=jax.ShapeDtypeStruct((BLOCK, HEADS * HD), bf16),
        in_specs=[smem] * (1 + most) + [anywhere] * 4,
        out_specs=vmem,
        scratch_shapes=[pltpu.VMEM((BLOCK, HEADS * HD), bf16)] * 3
        + [
            pltpu.SemaphoreType.DMA((3,)),
            pltpu.VMEM((slots, BLOCK, HD), bf16),
            pltpu.VMEM((rounds, half, BLOCK, HD), bf16),
            pltpu.SemaphoreType.DMA((slots, 2)),
            pltpu.SemaphoreType.DMA((rounds, group)),
            pltpu.SemaphoreType.DMA((rounds, half)),
            pltpu.SemaphoreType.DMA((slots,)),
        ]
        + [pltpu.VMEM((group, 3, BLOCK, HD), bf16)] * rounds,
        compiler_params=pltpu.CompilerParams(
            collective_id=number, has_side_effects=True, vmem_limit_bytes=60 << 20
        ),
    )(order, place, *picks, *rows, packed)


def body(queries, key_rows, value_rows, block_lists, block_counts):
    seq_count = lax.axis_size("seq")
    pair_count = lax.axis_size("pair")
    group = seq_count * pair_count
    most = block_lists.shape[2]
    heads = jnp.arange(HEADS, dtype=jnp.int32)
    active = jnp.max(block_counts, axis=1) > 1
    before = jnp.sum(
        jnp.where((heads[None, :] < heads[:, None]) & active[None, :], 1, 0), axis=1
    )
    place = jnp.where(active, before, -1).astype(jnp.int32)
    order = jnp.sum(
        jnp.where(place[None, :] == heads[:, None], heads[None, :], 0), axis=1
    ).astype(jnp.int32)
    filled = jnp.sum(active.astype(jnp.int32))
    picks = [
        jnp.where(block_counts > position, block_lists[:, :, position], -1).T
        for position in range(1, most)
    ]
    tables = (order, place, *picks)
    limits = jnp.asarray(SLOT_CHOICES[:-1], dtype=jnp.int32)
    branch = jnp.sum((filled > limits).astype(jnp.int32))
    return lax.switch(
        branch,
        [
            functools.partial(exchange, slots, number, seq_count, pair_count, most)
            for number, slots in enumerate(SLOT_CHOICES)
        ],
        tables,
        (queries, key_rows, value_rows),
    )


def solution(mesh):
    placed = P(("clips", "seq", "pair"), None)
    return jax.shard_map(
        body,
        mesh=mesh,
        in_specs=(placed, placed, placed, P(), P()),
        out_specs=placed,
        check_vma=False,
    )
```

```python
import functools
import math

import jax
import jax.numpy as jnp
from jax import lax
from jax.experimental import pallas as pl
from jax.experimental.pallas import tpu as pltpu
from jax.sharding import PartitionSpec as P

HEADS = 40
HD = 128
BLOCK = 128
MESH = pl.DeviceIdType.MESH
FEWEST = 15
SLOT_CHOICES = tuple(range(FEWEST, 28)) + (HEADS,)
SCALE = 1.0 / math.sqrt(HD)


def attend(query, key, value, live):
    scores = (
        lax.dot_general(
            query, key, (((1,), (1,)), ((), ())), preferred_element_type=jnp.float32
        )
        * SCALE
    )
    if live is not None:
        scores = jnp.where(live, scores, -1e30)
    raised = jnp.exp(scores - jnp.max(scores, axis=1, keepdims=True))
    total = jnp.sum(raised, axis=1, keepdims=True)
    mixed = jnp.dot(raised.astype(jnp.bfloat16), value, preferred_element_type=jnp.float32)
    return (mixed / total).astype(jnp.bfloat16)


def columns(head):
    return pl.ds(pl.multiple_of(head * HD, HD), HD)


def pack_kernel(slots, order_ref, q_ref, k_ref, v_ref, packed):
    def pack(slot, carry):
        cols = columns(order_ref[slot])
        packed[slot, 0] = q_ref[:, cols]
        packed[slot, 1] = k_ref[:, cols]
        packed[slot, 2] = v_ref[:, cols]
        return carry

    lax.fori_loop(0, slots, pack, 0, unroll=2)


def place_kernel(place_ref, alone_ref, returned, out_ref):
    def place(head, carry):
        at = place_ref[head]
        cols = columns(head)
        got = returned[jnp.maximum(at, 0)]
        out_ref[:, cols] = jnp.where(at >= 0, got, alone_ref[:, cols])
        return carry

    lax.fori_loop(0, HEADS, place, 0, unroll=4)


def kernel(
    slots,
    seq_count,
    pair_count,
    most,
    order_ref,
    *refs,
):
    picks = refs[: most - 1]
    (
        q_ref,
        k_ref,
        v_ref,
        packed,
        alone_ref,
        returned,
        mixed,
        send_sem,
        recv_sem,
        mixed_sem,
        returned_sem,
        *landed,
    ) = refs[most - 1 :]
    group = seq_count * pair_count
    half = group // 2
    rounds = -(-slots // half)
    clip = lax.axis_index("clips")
    me = lax.axis_index("seq") * pair_count + lax.axis_index("pair")
    side = me // half
    within = me % half
    crossed = half == 8 and pair_count == 4
    if crossed:
        plane, across = within // 4, within // 2 % 2
        turn = plane + 2 * ((plane + across) % 2) + 4 * (within % 2)
    else:
        turn = (within % (half // 2)) * 2 + within // (half // 2)

    def device(place):
        return (clip, place // pair_count, place % pair_count)

    def keeper(lane):
        if crossed:
            return (lane % 2) * 4 + (lane + lane // 2) % 2 * 2 + lane // 4
        return (lane % 2) * (half // 2) + lane // 2

    barrier = pltpu.get_barrier_semaphore()

    def greet(step, carry):
        pl.semaphore_signal(
            barrier, inc=1, device_id=device((me + step) % group), device_id_type=MESH
        )
        return carry

    lax.fori_loop(1, group, greet, 0)
    pl.semaphore_wait(barrier, group - 1)

    def far_copy(slot, row, owner):
        return pltpu.make_async_remote_copy(
            src_ref=packed.at[slot, pl.ds(1, 2)],
            dst_ref=landed[row].at[me, pl.ds(1, 2)],
            send_sem=send_sem.at[slot, 0],
            recv_sem=recv_sem.at[row, me],
            device_id=device(owner),
            device_id_type=MESH,
        )

    def near_copy(slot, row, owner):
        return pltpu.make_async_remote_copy(
            src_ref=packed.at[slot],
            dst_ref=landed[row].at[me],
            send_sem=send_sem.at[slot, 1],
            recv_sem=recv_sem.at[row, me],
            device_id=device(owner),
            device_id_type=MESH,
        )

    for row in range(rounds):
        width = min(half, slots - row * half)

        def give(step, carry, row=row, width=width):
            lane = (step + me) % width
            slot = row * half + lane
            far = (1 - side) * half + keeper(lane)
            near = side * half + keeper(lane)
            far_copy(slot, row, far).start()

            @pl.when(near != me)
            def _():
                near_copy(slot, row, near).start()

            @pl.when(near == me)
            def _():
                pltpu.make_async_copy(
                    packed.at[slot], landed[row].at[me], recv_sem.at[row, me]
                ).start()

            return carry

        lax.fori_loop(0, width, give, 0)

    def alone(head, carry):
        cols = columns(head)
        alone_ref[:, cols] = attend(q_ref[:, cols], k_ref[:, cols], v_ref[:, cols], None)
        return carry

    lax.fori_loop(0, HEADS, alone, 0, unroll=4)

    spot = lax.broadcasted_iota(jnp.int32, (BLOCK, most * BLOCK), 1)

    def back_copy(row, slot, near):
        return pltpu.make_async_remote_copy(
            src_ref=mixed.at[row, near],
            dst_ref=returned.at[slot],
            send_sem=mixed_sem.at[row, near],
            recv_sem=returned_sem.at[slot],
            device_id=device(side * half + near),
            device_id_type=MESH,
        )

    for row in range(rounds):
        slot = row * half + turn

        @pl.when(slot < slots)
        def _(row=row, slot=slot):
            def near_in(step, carry):
                source = side * half + step
                pltpu.make_async_copy(
                    landed[row].at[source], landed[row].at[source], recv_sem.at[row, source]
                ).wait()
                return carry

            lax.fori_loop(0, half, near_in, 0)

            def far_in(step, carry):
                source = (1 - side) * half + step
                got = landed[row].at[source, pl.ds(1, 2)]
                pltpu.make_async_copy(got, got, recv_sem.at[row, source]).wait()
                return carry

            lax.fori_loop(0, half, far_in, 0)

            head = order_ref[slot]

            def work(step, carry):
                near = (step + within + 1) % half
                block = side * half + near
                keys = [landed[row][block, 1]]
                values = [landed[row][block, 2]]
                live = 1
                for pick_ref in picks:
                    pick = pick_ref[block, head]
                    live += jnp.where(pick >= 0, 1, 0)
                    keys.append(landed[row][jnp.maximum(pick, 0), 1])
                    values.append(landed[row][jnp.maximum(pick, 0), 2])
                mixed[row, near] = attend(
                    landed[row][block, 0],
                    jnp.concatenate(keys, axis=0),
                    jnp.concatenate(values, axis=0),
                    spot < live * BLOCK,
                )

                @pl.when(near != within)
                def _():
                    back_copy(row, slot, near).start()

                @pl.when(near == within)
                def _():
                    pltpu.make_async_copy(
                        mixed.at[row, near], returned.at[slot], returned_sem.at[slot]
                    ).start()

                return carry

            lax.fori_loop(0, half, work, 0, unroll=4)

    def come(slot, carry):
        pltpu.make_async_copy(returned.at[slot], returned.at[slot], returned_sem.at[slot]).wait()
        return carry

    lax.fori_loop(0, slots, come, 0)

    for row in range(rounds):
        width = min(half, slots - row * half)

        def sent(lane, carry, row=row):
            slot = row * half + lane
            far = (1 - side) * half + keeper(lane)
            near = side * half + keeper(lane)
            far_copy(slot, row, far).wait_send()

            @pl.when(near != me)
            def _():
                near_copy(slot, row, near).wait_send()

            return carry

        lax.fori_loop(0, width, sent, 0)

        @pl.when(row * half + turn < slots)
        def _(row=row):
            def gone(step, carry):
                near = (step + within + 1) % half
                back_copy(row, row * half + turn, near).wait_send()
                return carry

            lax.fori_loop(0, half - 1, gone, 0)


def exchange(slots, number, seq_count, pair_count, most, tables, rows):
    group = seq_count * pair_count
    half = group // 2
    rounds = -(-slots // half)
    smem = pl.BlockSpec(memory_space=pltpu.SMEM)
    vmem = pl.BlockSpec(memory_space=pltpu.VMEM)
    bf16 = jnp.bfloat16
    order, place, *picks = tables
    whole_rows = jax.ShapeDtypeStruct((BLOCK, HEADS * HD), bf16)
    packed = pl.pallas_call(
        functools.partial(pack_kernel, slots),
        out_shape=jax.ShapeDtypeStruct((slots, 3, BLOCK, HD), bf16),
        in_specs=[smem] + [vmem] * 3,
        out_specs=vmem,
        compiler_params=pltpu.CompilerParams(vmem_limit_bytes=32 << 20),
    )(order, *rows)
    alone, returned = pl.pallas_call(
        functools.partial(kernel, slots, seq_count, pair_count, most),
        out_shape=(whole_rows, jax.ShapeDtypeStruct((slots, BLOCK, HD), bf16)),
        in_specs=[smem] * most + [vmem] * 3 + [pl.BlockSpec(memory_space=pl.ANY)],
        out_specs=(vmem, vmem),
        scratch_shapes=[
            pltpu.VMEM((rounds, half, BLOCK, HD), bf16),
            pltpu.SemaphoreType.DMA((slots, 2)),
            pltpu.SemaphoreType.DMA((rounds, group)),
            pltpu.SemaphoreType.DMA((rounds, half)),
            pltpu.SemaphoreType.DMA((slots,)),
        ]
        + [pltpu.VMEM((group, 3, BLOCK, HD), bf16)] * rounds,
        compiler_params=pltpu.CompilerParams(
            collective_id=number, has_side_effects=True, vmem_limit_bytes=48 << 20
        ),
    )(order, *picks, *rows, packed)
    return pl.pallas_call(
        place_kernel,
        out_shape=whole_rows,
        in_specs=[smem] + [vmem] * 2,
        out_specs=vmem,
        compiler_params=pltpu.CompilerParams(vmem_limit_bytes=32 << 20),
    )(place, alone, returned)


def body(queries, key_rows, value_rows, block_lists, block_counts):
    seq_count = lax.axis_size("seq")
    pair_count = lax.axis_size("pair")
    group = seq_count * pair_count
    most = block_lists.shape[2]
    heads = jnp.arange(HEADS, dtype=jnp.int32)
    active = jnp.max(block_counts, axis=1) > 1
    before = jnp.sum(
        jnp.where((heads[None, :] < heads[:, None]) & active[None, :], 1, 0), axis=1
    )
    place = jnp.where(active, before, -1).astype(jnp.int32)
    order = jnp.sum(
        jnp.where(place[None, :] == heads[:, None], heads[None, :], 0), axis=1
    ).astype(jnp.int32)
    filled = jnp.sum(active.astype(jnp.int32))
    picks = [
        jnp.where(block_counts > position, block_lists[:, :, position], -1).T
        for position in range(1, most)
    ]
    tables = (order, place, *picks)
    return lax.switch(
        filled - FEWEST,
        [
            functools.partial(exchange, slots, number, seq_count, pair_count, most)
            for number, slots in enumerate(SLOT_CHOICES)
        ],
        tables,
        (queries, key_rows, value_rows),
    )


def solution(mesh):
    placed = P(("clips", "seq", "pair"), None)
    return jax.shard_map(
        body,
        mesh=mesh,
        in_specs=(placed, placed, placed, P(), P()),
        out_specs=placed,
        check_vma=False,
    )
```

```python
import functools
import math

import jax
import jax.numpy as jnp
from jax import lax
from jax.experimental import pallas as pl
from jax.experimental.pallas import tpu as pltpu
from jax.sharding import PartitionSpec as P

HEADS = 40
HD = 128
BLOCK = 128
MESH = pl.DeviceIdType.MESH
FEWEST = 16
SLOT_CHOICES = tuple(range(FEWEST, 27, 2)) + (HEADS,)
SCALE = 1.0 / math.sqrt(HD)


def attend(query, key, value, live):
    scores = (
        lax.dot_general(
            query, key, (((1,), (1,)), ((), ())), preferred_element_type=jnp.float32
        )
        * SCALE
    )
    if live is not None:
        scores = jnp.where(live, scores, -1e30)
    raised = jnp.exp(scores - jnp.max(scores, axis=1, keepdims=True))
    total = jnp.sum(raised, axis=1, keepdims=True)
    mixed = jnp.dot(raised.astype(jnp.bfloat16), value, preferred_element_type=jnp.float32)
    return (mixed / total).astype(jnp.bfloat16)


def columns(head):
    return pl.ds(pl.multiple_of(head * HD, HD), HD)


def place_kernel(place_ref, alone_ref, returned, out_ref):
    def place(head, carry):
        at = place_ref[head]
        cols = columns(head)
        got = returned[jnp.maximum(at, 0)]
        out_ref[:, cols] = jnp.where(at >= 0, got, alone_ref[:, cols])
        return carry

    lax.fori_loop(0, HEADS, place, 0, unroll=4)


def kernel(
    slots,
    seq_count,
    pair_count,
    most,
    order_ref,
    lists_ref,
    counts_ref,
    q_ref,
    k_ref,
    v_ref,
    alone_ref,
    returned,
    mixed,
    spread,
    packed,
    send_sem,
    recv_sem,
    mixed_sem,
    returned_sem,
    *landed,
):
    group = seq_count * pair_count
    half = group // 2
    rounds = -(-slots // half)
    clip = lax.axis_index("clips")
    me = lax.axis_index("seq") * pair_count + lax.axis_index("pair")
    side = me // half
    within = me % half
    crossed = half == 8 and pair_count == 4
    if crossed:
        plane, across = within // 4, within // 2 % 2
        turn = plane + 2 * ((plane + across) % 2) + 4 * (within % 2)
    else:
        turn = (within % (half // 2)) * 2 + within // (half // 2)

    def device(place):
        return (clip, place // pair_count, place % pair_count)

    def keeper(lane):
        if crossed:
            return (lane % 2) * 4 + (lane + lane // 2) % 2 * 2 + lane // 4
        return (lane % 2) * (half // 2) + lane // 2

    barrier = pltpu.get_barrier_semaphore()

    def greet(step, carry):
        pl.semaphore_signal(
            barrier, inc=1, device_id=device((me + step) % group), device_id_type=MESH
        )
        return carry

    lax.fori_loop(1, group, greet, 0)

    def spread_head(head, carry):
        for part, ref in enumerate((q_ref, k_ref, v_ref)):
            spread[part, head] = ref[:, columns(head)]
        return carry

    lax.fori_loop(0, HEADS, spread_head, 0, unroll=4)
    pl.semaphore_wait(barrier, group - 1)

    def far_copy(slot, row, owner):
        return pltpu.make_async_remote_copy(
            src_ref=packed.at[slot, pl.ds(1, 2)],
            dst_ref=landed[row].at[me, pl.ds(1, 2)],
            send_sem=send_sem.at[slot, 0],
            recv_sem=recv_sem.at[row, me],
            device_id=device(owner),
            device_id_type=MESH,
        )

    def near_copy(slot, row, owner):
        return pltpu.make_async_remote_copy(
            src_ref=packed.at[slot],
            dst_ref=landed[row].at[me],
            send_sem=send_sem.at[slot, 1],
            recv_sem=recv_sem.at[row, me],
            device_id=device(owner),
            device_id_type=MESH,
        )

    def alone(head, carry):
        alone_ref[:, columns(head)] = attend(
            spread[0, head], spread[1, head], spread[2, head], None
        )
        return carry

    def sent(row, lane):
        slot = row * half + lane
        near = side * half + keeper(lane)
        far_copy(slot, row, (1 - side) * half + keeper(lane)).wait_send()

        @pl.when(near != me)
        def _():
            near_copy(slot, row, near).wait_send()

    widths = [min(half, slots - row * half) for row in range(rounds)]
    share = -(-HEADS // half)

    def give_row(row):
        def give(step, carry):
            if row == 1:
                first = step * share
                lax.fori_loop(first, jnp.minimum(first + share, HEADS), alone, 0)
            if row >= 1:
                sent(row - 1, (step + me) % half)
            lane = (step + me) % widths[row]
            slot = row * half + lane
            head = order_ref[slot]
            for part in range(3):
                packed[slot, part] = spread[part, head]
            far = (1 - side) * half + keeper(lane)
            near = side * half + keeper(lane)
            far_copy(slot, row, far).start()

            @pl.when(near != me)
            def _():
                near_copy(slot, row, near).start()

            @pl.when(near == me)
            def _():
                pltpu.make_async_copy(
                    packed.at[slot], landed[row].at[me], recv_sem.at[row, me]
                ).start()

            return carry

        lax.fori_loop(0, widths[row], give, 0)
        if row == min(1, rounds - 1):
            done = widths[row] * share if row == 1 else 0
            lax.fori_loop(min(done, HEADS), HEADS, alone, 0)

    spot = lax.broadcasted_iota(jnp.int32, (BLOCK, most * BLOCK), 1)

    def back_copy(row, slot, near):
        return pltpu.make_async_remote_copy(
            src_ref=mixed.at[row, near],
            dst_ref=returned.at[slot],
            send_sem=mixed_sem.at[row, near],
            recv_sem=returned_sem.at[slot],
            device_id=device(side * half + near),
            device_id_type=MESH,
        )

    def work_row(row):
        slot = row * half + turn

        @pl.when(slot < slots)
        def _():
            def near_in(step, carry):
                source = side * half + step
                pltpu.make_async_copy(
                    landed[row].at[source], landed[row].at[source], recv_sem.at[row, source]
                ).wait()
                return carry

            lax.fori_loop(0, half, near_in, 0)

            def far_in(step, carry):
                source = (1 - side) * half + step
                got = landed[row].at[source, pl.ds(1, 2)]
                pltpu.make_async_copy(got, got, recv_sem.at[row, source]).wait()
                return carry

            lax.fori_loop(0, half, far_in, 0)

            head = order_ref[slot]

            def work(step, carry):
                near = (step + within + 1) % half
                block = side * half + near
                keys = [landed[row][block, 1]]
                values = [landed[row][block, 2]]
                for position in range(1, most):
                    if len(lists_ref.shape) == 3:
                        pick = lists_ref[block, position, head]
                    else:
                        pick = lists_ref[(head * group + block) * most + position]
                    keys.append(landed[row][pick, 1])
                    values.append(landed[row][pick, 2])
                mixed[row, near] = attend(
                    landed[row][block, 0],
                    jnp.concatenate(keys, axis=0),
                    jnp.concatenate(values, axis=0),
                    spot < counts_ref[block, head] * BLOCK,
                )

                @pl.when(near != within)
                def _():
                    back_copy(row, slot, near).start()

                @pl.when(near == within)
                def _():
                    pltpu.make_async_copy(
                        mixed.at[row, near], returned.at[slot], returned_sem.at[slot]
                    ).start()

                return carry

            lax.fori_loop(0, half, work, 0, unroll=4)

    for row in range(rounds):
        give_row(row)
        if row >= 1:
            work_row(row - 1)
    work_row(rounds - 1)

    def come(slot, carry):
        pltpu.make_async_copy(returned.at[slot], returned.at[slot], returned_sem.at[slot]).wait()
        return carry

    lax.fori_loop(0, slots, come, 0)

    def last_sent(step, carry):
        sent(rounds - 1, (step + me) % widths[-1])
        return carry

    lax.fori_loop(0, widths[-1], last_sent, 0)
    if rounds > 1:

        def late_sent(step, carry):
            sent(rounds - 2, (step + me) % half)
            return carry

        lax.fori_loop(widths[-1], half, late_sent, 0)

    for row in range(rounds):

        @pl.when(row * half + turn < slots)
        def _(row=row):
            def gone(step, carry):
                near = (step + within + 1) % half
                back_copy(row, row * half + turn, near).wait_send()
                return carry

            lax.fori_loop(0, half - 1, gone, 0)


def exchange(slots, number, seq_count, pair_count, most, tables, rows):
    group = seq_count * pair_count
    half = group // 2
    rounds = -(-slots // half)
    smem = pl.BlockSpec(memory_space=pltpu.SMEM)
    vmem = pl.BlockSpec(memory_space=pltpu.VMEM)
    bf16 = jnp.bfloat16
    order, place, lists, counts = tables
    whole_rows = jax.ShapeDtypeStruct((BLOCK, HEADS * HD), bf16)
    alone, returned = pl.pallas_call(
        functools.partial(kernel, slots, seq_count, pair_count, most),
        out_shape=(whole_rows, jax.ShapeDtypeStruct((slots, BLOCK, HD), bf16)),
        in_specs=[smem] * 3 + [vmem] * 3,
        out_specs=(vmem, vmem),
        scratch_shapes=[
            pltpu.VMEM((rounds, half, BLOCK, HD), bf16),
            pltpu.VMEM((3, HEADS, BLOCK, HD), bf16),
            pltpu.VMEM((slots, 3, BLOCK, HD), bf16),
            pltpu.SemaphoreType.DMA((slots, 2)),
            pltpu.SemaphoreType.DMA((rounds, group)),
            pltpu.SemaphoreType.DMA((rounds, half)),
            pltpu.SemaphoreType.DMA((slots,)),
        ]
        + [pltpu.VMEM((group, 3, BLOCK, HD), bf16)] * rounds,
        compiler_params=pltpu.CompilerParams(
            collective_id=number, has_side_effects=True, vmem_limit_bytes=48 << 20
        ),
    )(order, lists, counts, *rows)
    return pl.pallas_call(
        place_kernel,
        out_shape=whole_rows,
        in_specs=[smem] + [vmem] * 2,
        out_specs=vmem,
        compiler_params=pltpu.CompilerParams(vmem_limit_bytes=32 << 20),
    )(place, alone, returned)


def body(queries, key_rows, value_rows, block_lists, block_counts):
    seq_count = lax.axis_size("seq")
    pair_count = lax.axis_size("pair")
    group = seq_count * pair_count
    most = block_lists.shape[2]
    heads = jnp.arange(HEADS, dtype=jnp.int32)
    active = jnp.max(block_counts, axis=1) > 1
    before = jnp.sum(
        jnp.where((heads[None, :] < heads[:, None]) & active[None, :], 1, 0), axis=1
    )
    place = jnp.where(active, before, -1).astype(jnp.int32)
    order = jnp.sum(
        jnp.where(place[None, :] == heads[:, None], heads[None, :], 0), axis=1
    ).astype(jnp.int32)
    filled = jnp.sum(active.astype(jnp.int32))
    small = group * most <= 64
    lists = block_lists.transpose(1, 2, 0) if small else block_lists.reshape(-1)
    tables = (order, place, lists, block_counts.T)
    return lax.switch(
        (filled - FEWEST + 1) // 2,
        [
            functools.partial(exchange, slots, number, seq_count, pair_count, most)
            for number, slots in enumerate(SLOT_CHOICES)
        ],
        tables,
        (queries, key_rows, value_rows),
    )


def solution(mesh):
    placed = P(("clips", "seq", "pair"), None)
    return jax.shard_map(
        body,
        mesh=mesh,
        in_specs=(placed, placed, placed, P(), P()),
        out_specs=placed,
        check_vma=False,
    )
```

```python
import functools
import math

import jax
import jax.numpy as jnp
from jax import lax
from jax.experimental import pallas as pl
from jax.experimental.pallas import tpu as pltpu
from jax.sharding import PartitionSpec as P

HEADS = 40
HD = 128
BLOCK = 128
MESH = pl.DeviceIdType.MESH
FEWEST = 16
SLOT_CHOICES = tuple(range(FEWEST, 29, 2)) + (HEADS,)
SCALE = 1.0 / math.sqrt(HD)


def attend(query, key, value, live):
    scores = (
        lax.dot_general(
            query, key, (((1,), (1,)), ((), ())), preferred_element_type=jnp.float32
        )
        * SCALE
    )
    if live is not None:
        scores = jnp.where(live, scores, -1e30)
    raised = jnp.exp(scores - jnp.max(scores, axis=1, keepdims=True))
    total = jnp.sum(raised, axis=1, keepdims=True)
    mixed = jnp.dot(raised.astype(jnp.bfloat16), value, preferred_element_type=jnp.float32)
    return (mixed / total).astype(jnp.bfloat16)


def columns(head):
    return pl.ds(pl.multiple_of(head * HD, HD), HD)


def place_kernel(parts, place_ref, alone_ref, returned, out_ref, rows_ref, sem):
    heads = HEADS // parts
    copies = []
    for part in range(parts):

        def place(head, carry):
            at = place_ref[head]
            cols = columns(head)
            got = returned[jnp.maximum(at, 0)]
            rows_ref[:, cols] = jnp.where(at >= 0, got, alone_ref[:, cols])
            return carry

        lax.fori_loop(part * heads, (part + 1) * heads, place, 0, unroll=2)
        cols = pl.ds(part * heads * HD, heads * HD)
        copies.append(
            pltpu.make_async_copy(rows_ref.at[:, cols], out_ref.at[:, cols], sem.at[part])
        )
        copies[-1].start()
    for copy in copies:
        copy.wait()


def kernel(
    slots,
    seq_count,
    pair_count,
    most,
    order_ref,
    lists_ref,
    counts_ref,
    q_hbm,
    k_hbm,
    v_hbm,
    alone_ref,
    returned,
    mixed,
    q_ref,
    k_ref,
    v_ref,
    own_sem,
    spread,
    packed,
    send_sem,
    recv_sem,
    mixed_sem,
    returned_sem,
    *landed,
):
    group = seq_count * pair_count
    half = group // 2
    rounds = -(-slots // half)
    clip = lax.axis_index("clips")
    me = lax.axis_index("seq") * pair_count + lax.axis_index("pair")
    side = me // half
    within = me % half
    crossed = half == 8 and pair_count == 4
    if crossed:
        plane, across = within // 4, within // 2 % 2
        turn = plane + 2 * ((plane + across) % 2) + 4 * (within % 2)
    else:
        turn = (within % (half // 2)) * 2 + within // (half // 2)

    def device(place):
        return (clip, place // pair_count, place % pair_count)

    def keeper(lane):
        if crossed:
            return (lane % 2) * 4 + (lane + lane // 2) % 2 * 2 + lane // 4
        return (lane % 2) * (half // 2) + lane // 2

    own_copies = [
        pltpu.make_async_copy(source, target, own_sem.at[part])
        for part, (source, target) in enumerate(((q_hbm, q_ref), (k_hbm, k_ref), (v_hbm, v_ref)))
    ]
    for copy in own_copies:
        copy.start()
    barrier = pltpu.get_barrier_semaphore()

    def greet(step, carry):
        pl.semaphore_signal(
            barrier, inc=1, device_id=device((me + step) % group), device_id_type=MESH
        )
        return carry

    lax.fori_loop(1, group, greet, 0)

    for copy in own_copies:
        copy.wait()

    def spread_head(head, carry):
        for part, ref in enumerate((q_ref, k_ref, v_ref)):
            spread[part, head] = ref[:, columns(head)]
        return carry

    lax.fori_loop(0, HEADS, spread_head, 0, unroll=4)
    pl.semaphore_wait(barrier, group - 1)

    def far_copy(slot, row, owner):
        return pltpu.make_async_remote_copy(
            src_ref=packed.at[slot, pl.ds(1, 2)],
            dst_ref=landed[row].at[me, pl.ds(1, 2)],
            send_sem=send_sem.at[slot, 0],
            recv_sem=recv_sem.at[row, me],
            device_id=device(owner),
            device_id_type=MESH,
        )

    def near_copy(slot, row, owner):
        return pltpu.make_async_remote_copy(
            src_ref=packed.at[slot],
            dst_ref=landed[row].at[me],
            send_sem=send_sem.at[slot, 1],
            recv_sem=recv_sem.at[row, me],
            device_id=device(owner),
            device_id_type=MESH,
        )

    def alone(head, carry):
        alone_ref[:, columns(head)] = attend(
            spread[0, head], spread[1, head], spread[2, head], None
        )
        return carry

    def sent(row, lane):
        slot = row * half + lane
        near = side * half + keeper(lane)
        far_copy(slot, row, (1 - side) * half + keeper(lane)).wait_send()

        @pl.when(near != me)
        def _():
            near_copy(slot, row, near).wait_send()

    widths = [min(half, slots - row * half) for row in range(rounds)]
    share = -(-HEADS // half)

    def give_row(row):
        def give(step, carry):
            if row == 1:
                first = step * share
                lax.fori_loop(first, jnp.minimum(first + share, HEADS), alone, 0)
            if row >= 1:
                sent(row - 1, (step + me) % half)
            lane = (step + me) % widths[row]
            slot = row * half + lane
            head = order_ref[slot]
            for part in range(3):
                packed[slot, part] = spread[part, head]
            far = (1 - side) * half + keeper(lane)
            near = side * half + keeper(lane)
            far_copy(slot, row, far).start()

            @pl.when(near != me)
            def _():
                near_copy(slot, row, near).start()

            @pl.when(near == me)
            def _():
                pltpu.make_async_copy(
                    packed.at[slot], landed[row].at[me], recv_sem.at[row, me]
                ).start()

            return carry

        lax.fori_loop(0, widths[row], give, 0)
        if row == min(1, rounds - 1):
            done = widths[row] * share if row == 1 else 0
            lax.fori_loop(min(done, HEADS), HEADS, alone, 0)

    spot = lax.broadcasted_iota(jnp.int32, (BLOCK, most * BLOCK), 1)

    def back_copy(row, slot, near):
        return pltpu.make_async_remote_copy(
            src_ref=mixed.at[row, near],
            dst_ref=returned.at[slot],
            send_sem=mixed_sem.at[row, near],
            recv_sem=returned_sem.at[slot],
            device_id=device(side * half + near),
            device_id_type=MESH,
        )

    def work_row(row):
        slot = row * half + turn

        @pl.when(slot < slots)
        def _():
            def near_in(step, carry):
                source = side * half + step
                pltpu.make_async_copy(
                    landed[row].at[source], landed[row].at[source], recv_sem.at[row, source]
                ).wait()
                return carry

            lax.fori_loop(0, half, near_in, 0)

            def far_in(step, carry):
                source = (1 - side) * half + step
                got = landed[row].at[source, pl.ds(1, 2)]
                pltpu.make_async_copy(got, got, recv_sem.at[row, source]).wait()
                return carry

            lax.fori_loop(0, half, far_in, 0)

            head = order_ref[slot]

            def work(step, carry):
                near = (step + within + 1) % half
                block = side * half + near
                keys = [landed[row][block, 1]]
                values = [landed[row][block, 2]]
                for position in range(1, most):
                    if len(lists_ref.shape) == 3:
                        pick = lists_ref[block, position, head]
                    else:
                        pick = lists_ref[(head * group + block) * most + position]
                    keys.append(landed[row][pick, 1])
                    values.append(landed[row][pick, 2])
                mixed[row, near] = attend(
                    landed[row][block, 0],
                    jnp.concatenate(keys, axis=0),
                    jnp.concatenate(values, axis=0),
                    spot < counts_ref[block, head] * BLOCK,
                )

                @pl.when(near != within)
                def _():
                    back_copy(row, slot, near).start()

                @pl.when(near == within)
                def _():
                    pltpu.make_async_copy(
                        mixed.at[row, near], returned.at[slot], returned_sem.at[slot]
                    ).start()

                return carry

            lax.fori_loop(0, half, work, 0, unroll=4)

    for row in range(rounds):
        give_row(row)
        if row >= 1:
            work_row(row - 1)
    work_row(rounds - 1)

    def come(slot, carry):
        pltpu.make_async_copy(returned.at[slot], returned.at[slot], returned_sem.at[slot]).wait()
        return carry

    lax.fori_loop(0, slots, come, 0)

    def last_sent(step, carry):
        sent(rounds - 1, (step + me) % widths[-1])
        return carry

    lax.fori_loop(0, widths[-1], last_sent, 0)
    if rounds > 1:

        def late_sent(step, carry):
            sent(rounds - 2, (step + me) % half)
            return carry

        lax.fori_loop(widths[-1], half, late_sent, 0)

    for row in range(rounds):

        @pl.when(row * half + turn < slots)
        def _(row=row):
            def gone(step, carry):
                near = (step + within + 1) % half
                back_copy(row, row * half + turn, near).wait_send()
                return carry

            lax.fori_loop(0, half - 1, gone, 0)


def exchange(slots, number, seq_count, pair_count, most, tables, rows):
    group = seq_count * pair_count
    half = group // 2
    rounds = -(-slots // half)
    smem = pl.BlockSpec(memory_space=pltpu.SMEM)
    vmem = pl.BlockSpec(memory_space=pltpu.VMEM)
    bf16 = jnp.bfloat16
    order, lists, counts = tables
    whole_rows = jax.ShapeDtypeStruct((BLOCK, HEADS * HD), bf16)
    return pl.pallas_call(
        functools.partial(kernel, slots, seq_count, pair_count, most),
        out_shape=(whole_rows, jax.ShapeDtypeStruct((HEADS, BLOCK, HD), bf16)),
        in_specs=[smem] * 3 + [pl.BlockSpec(memory_space=pltpu.HBM)] * 3,
        out_specs=(vmem, vmem),
        scratch_shapes=[
            pltpu.VMEM((rounds, half, BLOCK, HD), bf16),
            *[pltpu.VMEM((BLOCK, HEADS * HD), bf16)] * 3,
            pltpu.SemaphoreType.DMA((3,)),
            pltpu.VMEM((3, HEADS, BLOCK, HD), bf16),
            pltpu.VMEM((slots, 3, BLOCK, HD), bf16),
            pltpu.SemaphoreType.DMA((slots, 2)),
            pltpu.SemaphoreType.DMA((rounds, group)),
            pltpu.SemaphoreType.DMA((rounds, half)),
            pltpu.SemaphoreType.DMA((slots,)),
        ]
        + [pltpu.VMEM((group, 3, BLOCK, HD), bf16)] * rounds,
        compiler_params=pltpu.CompilerParams(
            collective_id=number, has_side_effects=True, vmem_limit_bytes=48 << 20
        ),
    )(order, lists, counts, *rows)

def body(queries, key_rows, value_rows, block_lists, block_counts):
    seq_count = lax.axis_size("seq")
    pair_count = lax.axis_size("pair")
    group = seq_count * pair_count
    most = block_lists.shape[2]
    heads = jnp.arange(HEADS, dtype=jnp.int32)
    active = jnp.max(block_counts, axis=1) > 1
    before = jnp.sum(
        jnp.where((heads[None, :] < heads[:, None]) & active[None, :], 1, 0), axis=1
    )
    place = jnp.where(active, before, -1).astype(jnp.int32)
    order = jnp.sum(
        jnp.where(place[None, :] == heads[:, None], heads[None, :], 0), axis=1
    ).astype(jnp.int32)
    filled = jnp.sum(active.astype(jnp.int32))
    small = group * most <= 64
    lists = block_lists.transpose(1, 2, 0) if small else block_lists.reshape(-1)
    tables = (order, lists, block_counts.T)
    alone, returned = lax.switch(
        (filled - FEWEST + 1) // 2,
        [
            functools.partial(exchange, slots, number, seq_count, pair_count, most)
            for number, slots in enumerate(SLOT_CHOICES)
        ],
        tables,
        (queries, key_rows, value_rows),
    )
    parts = 4
    return pl.pallas_call(
        functools.partial(place_kernel, parts),
        out_shape=jax.ShapeDtypeStruct((BLOCK, HEADS * HD), jnp.bfloat16),
        in_specs=[pl.BlockSpec(memory_space=pltpu.SMEM)]
        + [pl.BlockSpec(memory_space=pltpu.VMEM)] * 2,
        out_specs=pl.BlockSpec(memory_space=pltpu.HBM),
        scratch_shapes=[
            pltpu.VMEM((BLOCK, HEADS * HD), jnp.bfloat16),
            pltpu.SemaphoreType.DMA((parts,)),
        ],
        compiler_params=pltpu.CompilerParams(vmem_limit_bytes=32 << 20),
    )(place, alone, returned)


def solution(mesh):
    placed = P(("clips", "seq", "pair"), None)
    return jax.shard_map(
        body,
        mesh=mesh,
        in_specs=(placed, placed, placed, P(), P()),
        out_specs=placed,
        check_vma=False,
    )
```

```python
import functools
import math

import jax
import jax.numpy as jnp
from jax import lax
from jax.experimental import pallas as pl
from jax.experimental.pallas import tpu as pltpu
from jax.sharding import PartitionSpec as P

HEADS = 40
HD = 128
BLOCK = 128
MESH = pl.DeviceIdType.MESH
SLOT_CHOICES = (16, 18, 19, 20, 21, 22, 23, 24, 26, 28, HEADS)
SCALE = 1.0 / math.sqrt(HD)


def attend(query, key, value, live):
    scores = (
        lax.dot_general(
            query, key, (((1,), (1,)), ((), ())), preferred_element_type=jnp.float32
        )
        * SCALE
    )
    if live is not None:
        scores = jnp.where(live, scores, -1e30)
    raised = jnp.exp(scores - jnp.max(scores, axis=1, keepdims=True))
    total = jnp.sum(raised, axis=1, keepdims=True)
    mixed = jnp.dot(raised.astype(jnp.bfloat16), value, preferred_element_type=jnp.float32)
    return (mixed / total).astype(jnp.bfloat16)


def columns(head):
    return pl.ds(pl.multiple_of(head * HD, HD), HD)


def place_kernel(parts, place_ref, alone_ref, returned, out_ref, rows_ref, sem):
    heads = HEADS // parts
    copies = []
    for part in range(parts):

        def place(head, carry):
            at = place_ref[head]
            cols = columns(head)
            got = returned[jnp.maximum(at, 0)]
            rows_ref[:, cols] = jnp.where(at >= 0, got, alone_ref[:, cols])
            return carry

        lax.fori_loop(part * heads, (part + 1) * heads, place, 0, unroll=2)
        cols = pl.ds(part * heads * HD, heads * HD)
        copies.append(
            pltpu.make_async_copy(rows_ref.at[:, cols], out_ref.at[:, cols], sem.at[part])
        )
        copies[-1].start()
    for copy in copies:
        copy.wait()


def kernel(
    slots,
    seq_count,
    pair_count,
    most,
    order_ref,
    lists_ref,
    counts_ref,
    q_hbm,
    k_hbm,
    v_hbm,
    alone_ref,
    returned,
    mixed,
    q_ref,
    k_ref,
    v_ref,
    own_sem,
    spread,
    packed,
    send_sem,
    recv_sem,
    mixed_sem,
    returned_sem,
    *landed,
):
    group = seq_count * pair_count
    half = group // 2
    rounds = -(-slots // half)
    clip = lax.axis_index("clips")
    me = lax.axis_index("seq") * pair_count + lax.axis_index("pair")
    side = me // half
    within = me % half
    crossed = half == 8 and pair_count == 4
    if crossed:
        plane, across = within // 4, within // 2 % 2
        turn = plane + 2 * ((plane + across) % 2) + 4 * (within % 2)
    else:
        turn = (within % (half // 2)) * 2 + within // (half // 2)

    def device(place):
        return (clip, place // pair_count, place % pair_count)

    def keeper(lane):
        if crossed:
            return (lane % 2) * 4 + (lane + lane // 2) % 2 * 2 + lane // 4
        return (lane % 2) * (half // 2) + lane // 2

    own_copies = [
        pltpu.make_async_copy(source, target, own_sem.at[part])
        for part, (source, target) in enumerate(((q_hbm, q_ref), (k_hbm, k_ref), (v_hbm, v_ref)))
    ]
    for copy in own_copies:
        copy.start()
    barrier = pltpu.get_barrier_semaphore()

    def greet(step, carry):
        pl.semaphore_signal(
            barrier, inc=1, device_id=device((me + step) % group), device_id_type=MESH
        )
        return carry

    lax.fori_loop(1, group, greet, 0)

    for copy in own_copies:
        copy.wait()

    def spread_head(head, carry):
        for part, ref in enumerate((q_ref, k_ref, v_ref)):
            spread[part, head] = ref[:, columns(head)]
        return carry

    lax.fori_loop(0, HEADS, spread_head, 0, unroll=4)
    pl.semaphore_wait(barrier, group - 1)

    def far_copy(slot, row, owner):
        return pltpu.make_async_remote_copy(
            src_ref=packed.at[slot, pl.ds(1, 2)],
            dst_ref=landed[row].at[me, pl.ds(1, 2)],
            send_sem=send_sem.at[slot, 0],
            recv_sem=recv_sem.at[row, me],
            device_id=device(owner),
            device_id_type=MESH,
        )

    def near_copy(slot, row, owner):
        return pltpu.make_async_remote_copy(
            src_ref=packed.at[slot],
            dst_ref=landed[row].at[me],
            send_sem=send_sem.at[slot, 1],
            recv_sem=recv_sem.at[row, me],
            device_id=device(owner),
            device_id_type=MESH,
        )

    def alone(head, carry):
        alone_ref[:, columns(head)] = attend(
            spread[0, head], spread[1, head], spread[2, head], None
        )
        return carry

    def sent(row, lane):
        slot = row * half + lane
        near = side * half + keeper(lane)
        far_copy(slot, row, (1 - side) * half + keeper(lane)).wait_send()

        @pl.when(near != me)
        def _():
            near_copy(slot, row, near).wait_send()

    widths = [min(half, slots - row * half) for row in range(rounds)]
    share = -(-HEADS // half)

    def give_row(row):
        def give(step, carry):
            if row == 1:
                first = step * share
                lax.fori_loop(first, jnp.minimum(first + share, HEADS), alone, 0)
            if row >= 1:
                sent(row - 1, (step + me) % half)
            lane = (step + me) % widths[row]
            slot = row * half + lane
            head = order_ref[slot]
            for part in range(3):
                packed[slot, part] = spread[part, head]
            far = (1 - side) * half + keeper(lane)
            near = side * half + keeper(lane)
            far_copy(slot, row, far).start()

            @pl.when(near != me)
            def _():
                near_copy(slot, row, near).start()

            @pl.when(near == me)
            def _():
                pltpu.make_async_copy(
                    packed.at[slot], landed[row].at[me], recv_sem.at[row, me]
                ).start()

            return carry

        lax.fori_loop(0, widths[row], give, 0)
        if row == min(1, rounds - 1):
            done = widths[row] * share if row == 1 else 0
            lax.fori_loop(min(done, HEADS), HEADS, alone, 0)

    spot = lax.broadcasted_iota(jnp.int32, (BLOCK, most * BLOCK), 1)

    def back_copy(row, slot, near):
        return pltpu.make_async_remote_copy(
            src_ref=mixed.at[row, near],
            dst_ref=returned.at[slot],
            send_sem=mixed_sem.at[row, near],
            recv_sem=returned_sem.at[slot],
            device_id=device(side * half + near),
            device_id_type=MESH,
        )

    def work_row(row):
        slot = row * half + turn

        @pl.when(slot < slots)
        def _():
            def near_in(step, carry):
                source = side * half + step
                pltpu.make_async_copy(
                    landed[row].at[source], landed[row].at[source], recv_sem.at[row, source]
                ).wait()
                return carry

            lax.fori_loop(0, half, near_in, 0)

            def far_in(step, carry):
                source = (1 - side) * half + step
                got = landed[row].at[source, pl.ds(1, 2)]
                pltpu.make_async_copy(got, got, recv_sem.at[row, source]).wait()
                return carry

            lax.fori_loop(0, half, far_in, 0)

            head = order_ref[slot]

            def work(step, carry):
                near = (step + within + 1) % half
                block = side * half + near
                keys = [landed[row][block, 1]]
                values = [landed[row][block, 2]]
                for position in range(1, most):
                    if len(lists_ref.shape) == 3:
                        pick = lists_ref[block, position, head]
                    else:
                        pick = lists_ref[(head * group + block) * most + position]
                    keys.append(landed[row][pick, 1])
                    values.append(landed[row][pick, 2])
                mixed[row, near] = attend(
                    landed[row][block, 0],
                    jnp.concatenate(keys, axis=0),
                    jnp.concatenate(values, axis=0),
                    spot < counts_ref[block, head] * BLOCK,
                )

                @pl.when(near != within)
                def _():
                    back_copy(row, slot, near).start()

                @pl.when(near == within)
                def _():
                    pltpu.make_async_copy(
                        mixed.at[row, near], returned.at[slot], returned_sem.at[slot]
                    ).start()

                return carry

            lax.fori_loop(0, half, work, 0, unroll=4)

    for row in range(rounds):
        give_row(row)
        if row >= 1:
            work_row(row - 1)
    work_row(rounds - 1)

    def come(slot, carry):
        pltpu.make_async_copy(returned.at[slot], returned.at[slot], returned_sem.at[slot]).wait()
        return carry

    lax.fori_loop(0, slots, come, 0)

    def last_sent(step, carry):
        sent(rounds - 1, (step + me) % widths[-1])
        return carry

    lax.fori_loop(0, widths[-1], last_sent, 0)
    if rounds > 1:

        def late_sent(step, carry):
            sent(rounds - 2, (step + me) % half)
            return carry

        lax.fori_loop(widths[-1], half, late_sent, 0)

    for row in range(rounds):

        @pl.when(row * half + turn < slots)
        def _(row=row):
            def gone(step, carry):
                near = (step + within + 1) % half
                back_copy(row, row * half + turn, near).wait_send()
                return carry

            lax.fori_loop(0, half - 1, gone, 0)


def exchange(slots, number, seq_count, pair_count, most, tables, rows):
    group = seq_count * pair_count
    half = group // 2
    rounds = -(-slots // half)
    smem = pl.BlockSpec(memory_space=pltpu.SMEM)
    vmem = pl.BlockSpec(memory_space=pltpu.VMEM)
    bf16 = jnp.bfloat16
    order, lists, counts = tables
    whole_rows = jax.ShapeDtypeStruct((BLOCK, HEADS * HD), bf16)
    return pl.pallas_call(
        functools.partial(kernel, slots, seq_count, pair_count, most),
        out_shape=(whole_rows, jax.ShapeDtypeStruct((HEADS, BLOCK, HD), bf16)),
        in_specs=[smem] * 3 + [pl.BlockSpec(memory_space=pltpu.HBM)] * 3,
        out_specs=(vmem, vmem),
        scratch_shapes=[
            pltpu.VMEM((rounds, half, BLOCK, HD), bf16),
            *[pltpu.VMEM((BLOCK, HEADS * HD), bf16)] * 3,
            pltpu.SemaphoreType.DMA((3,)),
            pltpu.VMEM((3, HEADS, BLOCK, HD), bf16),
            pltpu.VMEM((slots, 3, BLOCK, HD), bf16),
            pltpu.SemaphoreType.DMA((slots, 2)),
            pltpu.SemaphoreType.DMA((rounds, group)),
            pltpu.SemaphoreType.DMA((rounds, half)),
            pltpu.SemaphoreType.DMA((slots,)),
        ]
        + [pltpu.VMEM((group, 3, BLOCK, HD), bf16)] * rounds,
        compiler_params=pltpu.CompilerParams(
            collective_id=number, has_side_effects=True, vmem_limit_bytes=48 << 20
        ),
    )(order, lists, counts, *rows)

def body(queries, key_rows, value_rows, block_lists, block_counts):
    seq_count = lax.axis_size("seq")
    pair_count = lax.axis_size("pair")
    group = seq_count * pair_count
    most = block_lists.shape[2]
    heads = jnp.arange(HEADS, dtype=jnp.int32)
    active = jnp.max(block_counts, axis=1) > 1
    before = jnp.sum(
        jnp.where((heads[None, :] < heads[:, None]) & active[None, :], 1, 0), axis=1
    )
    place = jnp.where(active, before, -1).astype(jnp.int32)
    order = jnp.sum(
        jnp.where(place[None, :] == heads[:, None], heads[None, :], 0), axis=1
    ).astype(jnp.int32)
    over = place == SLOT_CHOICES[0]
    for slots in SLOT_CHOICES[1:-1]:
        over |= place == slots
    branch = jnp.sum(over.astype(jnp.int32))
    small = group * most <= 64
    lists = block_lists.transpose(1, 2, 0) if small else block_lists.reshape(-1)
    tables = (order, lists, block_counts.T)
    alone, returned = lax.switch(
        branch,
        [
            functools.partial(exchange, slots, number, seq_count, pair_count, most)
            for number, slots in enumerate(SLOT_CHOICES)
        ],
        tables,
        (queries, key_rows, value_rows),
    )
    parts = 4
    return pl.pallas_call(
        functools.partial(place_kernel, parts),
        out_shape=jax.ShapeDtypeStruct((BLOCK, HEADS * HD), jnp.bfloat16),
        in_specs=[pl.BlockSpec(memory_space=pltpu.SMEM)]
        + [pl.BlockSpec(memory_space=pltpu.VMEM)] * 2,
        out_specs=pl.BlockSpec(memory_space=pltpu.HBM),
        scratch_shapes=[
            pltpu.VMEM((BLOCK, HEADS * HD), jnp.bfloat16),
            pltpu.SemaphoreType.DMA((parts,)),
        ],
        compiler_params=pltpu.CompilerParams(vmem_limit_bytes=32 << 20),
    )(place, alone, returned)


def solution(mesh):
    placed = P(("clips", "seq", "pair"), None)
    return jax.shard_map(
        body,
        mesh=mesh,
        in_specs=(placed, placed, placed, P(), P()),
        out_specs=placed,
        check_vma=False,
    )
```
